32 devices in a mesh: tm: 16 (over z, y, x), rows: 2 (over core).
Axes of the slice: x: 2, y: 2, z: 4, core: 2. Of those that a mesh axis runs over, the one named last changes fastest.
Arguments:
- band_blocks: float32 [8, 3, 64, 64], replicated, may hold values from 0.1 to 1
- band_offsets: int32 [8, 3], replicated, may hold values from 0 to 7, as said below
- retention: float32 [512], replicated, may hold values from 0.85 to 0.99
- frame_scale: float32 [64, 8], P('tm'), may hold values from 0.95 to 0.999
- sensor_index: int32 [128], replicated, may hold values from 0 to 511, as said below
- sensor_gain: float32 [128], replicated, may hold values from 0.2 to 0.6
- readings: float32 [64, 128], P('tm'), may hold values from -6 to 6
- noise_cov: float32 [512, 512], P(None, 'rows'), may hold values from -0.01 to 0.2
- initial_mean: float32 [512], replicated, may hold values from -6 to 6
- smoother_gain: float32 [512, 512], replicated, may hold values from -0.001 to 1, as said below
Outputs:
- filtered_cov: float32 [16, 512, 512], P('tm', None, 'rows')
- smoothed_means: float32 [64, 512], P('tm', 'rows')
The draws below stay inside these ranges and needn't reach their ends.
Inputs may be any that keep to these rules, and one draw needn't show every extreme that they name: `band_offsets`: band 0 of block row i names block i; the other bands of a row name distinct other blocks. `sensor_index`: the sensors read distinct nodes. Every eigenvalue of smoother_gain lies inside the unit circle.
All inputs are finite; a program needn't handle non-finite values.
Results may differ from the reference program's by a relative error of at most 0.0003.
Values sent between devices are 32-bit elements; how exact they have to be, the bound alone decides.
A program may use at most 64 MiB of HBM per device.

```python
import jax
import jax.numpy as jnp
from jax import lax

N = 512
BLK = 64
BANDS = 3
S = 128
FR_DEV = 4
NB = 8
FRAMES = 64
N_TM = 16


def sensor_nodes(key):
    return jax.random.permutation(jax.random.fold_in(key, 11), N)[:S].astype(jnp.int32)


def draw_band_offsets(key, part):
    block_count = N // BLK
    row_keys = jax.random.split(jax.random.fold_in(key, 41), block_count)

    def one_row(row_key):
        return jax.random.permutation(row_key, block_count - 1)[:BANDS - 1] + 1
    shifts = jax.vmap(one_row)(row_keys).astype(jnp.int32)
    block_rows = jnp.arange(block_count, dtype=jnp.int32)[:, None]
    others = (block_rows + shifts) % block_count
    return jnp.concatenate([block_rows, others], axis=1).astype(jnp.int32)


def draw_sensor_index(key, part):
    return sensor_nodes(key)


def draw_retention(key, part):
    key_high = jax.random.fold_in(jax.random.fold_in(key, 61), 1)
    values = jax.random.uniform(key_high, (N,), jnp.float32, 0.85, 0.99)
    return values.astype(jnp.float32)


def draw_frame_scale(key, part):
    frame_key = jax.random.fold_in(key, 51)
    values = jax.random.uniform(frame_key, (FRAMES, N // BLK), jnp.float32, 0.95, 0.999)
    return values.astype(jnp.float32)


def draw_sensor_gain(key, part):
    gain_key = jax.random.fold_in(key, 71)
    values = jax.random.uniform(gain_key, (S,), jnp.float32, 0.2, 0.6)
    return values.astype(jnp.float32)


def draw_noise_cov(key, part):
    key_spread, key_diag = jax.random.split(jax.random.fold_in(key, 21))
    spread = jax.random.uniform(key_spread, (N, N), jnp.float32, -1.0, 1.0)
    offdiag = 0.75 * (spread + spread.T) / N
    identity = jnp.eye(N, dtype=jnp.float32)
    diagonal_part = jax.random.uniform(key_diag, (N,), jnp.float32, 1.6, 3.0)
    values = 0.03 * (offdiag * (1.0 - identity) + identity * diagonal_part[:, None])
    return values.astype(jnp.float32)


def draw_smoother_gain(key, part):
    key_spread, key_slow, key_fast, key_pick = jax.random.split(jax.random.fold_in(key, 31), 4)
    slow_rates = jax.random.uniform(key_slow, (N,), jnp.float32, 0.2, 2.0)
    slow_part = jnp.exp(-slow_rates / (1.0 * FRAMES))
    fast_lengths = jax.random.uniform(key_fast, (N,), jnp.float32, 20.0, 50.0)
    fast_part = jnp.exp(-1.0 / fast_lengths)
    picks = jax.random.randint(key_pick, (N,), 0, 10)
    slow_count = 5
    diagonal_part = jnp.where(picks < slow_count, slow_part, fast_part)
    spread = jax.random.uniform(key_spread, (N, N), jnp.float32, -1.0, 1.0)
    offdiag = spread * (0.5 * (1.0 - diagonal_part)[:, None] / N)
    identity = jnp.eye(N, dtype=jnp.float32)
    return (offdiag * (1.0 - identity) + identity * diagonal_part[:, None]).astype(jnp.float32)


def levels(stream_key, shape, cuts, smallest, high):
    def one(position, parts):
        draws = jax.random.uniform(jax.random.fold_in(jax.random.fold_in(stream_key, 6), position), (parts,), jnp.float32, smallest / len(cuts), high / len(cuts))
        return jnp.repeat(jnp.exp(draws), shape[position] // parts).reshape((-1,) + (1,) * (len(shape) - position - 1))

    factor_of = one(*cuts[0])
    for cut in cuts[1:]:
        factor_of = factor_of * one(*cut)
    return factor_of


def noise(stream_key, shape, deviation, bound, shards=(), kind=jnp.bfloat16):
    gain = levels(stream_key, shape, shards, -0.22, 0.18) if shards else 1.0
    values = jax.random.normal(stream_key, shape, jnp.float32) * deviation * gain
    return jnp.minimum(jnp.maximum(values, -bound), bound).astype(kind)


def setup_inputs(seed: int = 0) -> dict:
    keys = jax.random.split(jax.random.key(seed), 11)
    band_blocks = jnp.clip(jax.random.uniform(keys[0], (NB, BANDS, BLK, BLK), jnp.float32, 0.1, 1.0), 0.1, 1.0)
    band_offsets = draw_band_offsets(jax.random.fold_in(keys[10], 71), 0)
    retention = draw_retention(jax.random.fold_in(keys[10], 71), 0)
    frame_scale = draw_frame_scale(jax.random.fold_in(keys[10], 71), 0)
    sensor_index = draw_sensor_index(jax.random.fold_in(keys[10], 71), 0)
    sensor_gain = draw_sensor_gain(jax.random.fold_in(keys[10], 71), 0)
    readings = noise(keys[6], (FRAMES, S), 1.0, 6.0, ((0, 16),), jnp.float32)
    noise_cov = draw_noise_cov(jax.random.fold_in(keys[10], 71), 0)
    initial_mean = noise(keys[8], (N,), 1.0, 6.0, (), jnp.float32)
    smoother_gain = draw_smoother_gain(jax.random.fold_in(keys[10], 71), 0)
    return dict(band_blocks=band_blocks, band_offsets=band_offsets, retention=retention, frame_scale=frame_scale, sensor_index=sensor_index, sensor_gain=sensor_gain, readings=readings, noise_cov=noise_cov, initial_mean=initial_mean, smoother_gain=smoother_gain)


HIGHEST_PRECISION = lax.Precision.HIGHEST


def build_coupling(band_blocks, band_offsets, retention):
    block_count = band_blocks.shape[0]
    block_size = band_blocks.shape[2]
    totals = jnp.sum(band_blocks, axis=(1, 3))
    normed = band_blocks / totals[:, None, :, None]
    placement = (band_offsets[:, :, None] == jnp.arange(block_count, dtype=jnp.int32)[None, None, :]).astype(jnp.float32)
    spread_matrix = jnp.einsum("ibj,ibac->iajc", placement, normed, precision=HIGHEST_PRECISION)
    spread_matrix = spread_matrix.reshape(block_count * block_size, block_count * block_size)
    return (1.0 - retention)[:, None] * spread_matrix + jnp.diag(retention)


def reference(band_blocks, band_offsets, retention, frame_scale, sensor_index, sensor_gain, readings, noise_cov, initial_mean, smoother_gain):
    coupling = build_coupling(band_blocks, band_offsets, retention)
    node_count = coupling.shape[0]
    sensor_hit = (sensor_index[:, None] == jnp.arange(node_count, dtype=jnp.int32)[None, :]).astype(jnp.float32)
    damping = 1.0 - jnp.dot(sensor_gain, sensor_hit, precision=HIGHEST_PRECISION)
    inject = jnp.dot(readings * sensor_gain[None, :], sensor_hit, precision=HIGHEST_PRECISION)

    def frame_step(carry, inputs):
        mean_now, cov_now = carry
        scale_row, injected = inputs
        transition = jnp.repeat(scale_row, BLK)[:, None] * coupling
        predicted = jnp.dot(transition, mean_now, precision=HIGHEST_PRECISION)
        update = damping[:, None] * transition
        mean_now = damping * predicted + injected
        cov_now = jnp.dot(jnp.dot(update, cov_now, precision=HIGHEST_PRECISION), update.T, precision=HIGHEST_PRECISION) + noise_cov
        return (mean_now, cov_now), (mean_now, predicted)

    def segment_step(carry, inputs):
        carry, stacks = lax.scan(frame_step, carry, inputs)
        return carry, (stacks[0], stacks[1], carry[1])

    scales = frame_scale.reshape(N_TM, FR_DEV, frame_scale.shape[1])
    injects = inject.reshape(N_TM, FR_DEV, node_count)
    start = (initial_mean, jnp.zeros((node_count, node_count), jnp.float32))
    _, (mean_stack, pred_stack, covs) = lax.scan(segment_step, start, (scales, injects))
    mean_stack = mean_stack.reshape(FRAMES, node_count)
    pred_stack = pred_stack.reshape(FRAMES, node_count)
    pred_after = jnp.concatenate([pred_stack[1:], jnp.zeros((1, node_count), jnp.float32)], axis=0)

    def back_wrap(smooth_next, inputs):
        mean_now, pred_next, is_last = inputs
        bracket = jnp.where(is_last, jnp.zeros_like(smooth_next), smooth_next - pred_next)
        smooth = mean_now + jnp.dot(smoother_gain, bracket, precision=HIGHEST_PRECISION)
        return smooth, smooth

    last_flags = jnp.arange(FRAMES, dtype=jnp.int32) == FRAMES - 1
    _, smoothed = lax.scan(back_wrap, jnp.zeros((node_count,), jnp.float32), (mean_stack, pred_after, last_flags), reverse=True)
    return covs, smoothed
```

```python
import functools

import jax
import jax.numpy as jnp
from jax import lax
from jax.experimental import pallas as pl
from jax.experimental.pallas import tpu as pltpu
from jax.sharding import PartitionSpec as P

F32 = jnp.float32
BF16 = jnp.bfloat16
NT = (((1,), (1,)), ((), ()))


def dot(left, right):
    return jnp.dot(left, right, preferred_element_type=F32)


def dot_nt(left, right):
    return lax.dot_general(left, right, NT, preferred_element_type=F32)


def split(value):
    high = value.astype(BF16)
    return high, (value - high.astype(F32)).astype(BF16)


def column(row, width=128):
    return jnp.transpose(jnp.broadcast_to(row, (width, row.shape[1])))


def kernel(
    where_ref, offsets_ref, scale_ref, blocks_ref, retention_ref, index_ref, gain_ref,
    scale_rows_ref, readings_ref, noise_ref, start_ref, smoother_ref,
    cov_ref, smooth_ref,
    spread_ref, left_ref, right_ref, cov_now, cov_half, inject_ref, pred_ref, innov_ref,
    power_ref,
):
    segment, panel = where_ref[0], where_ref[1]
    block_count, bands, size, _ = blocks_ref.shape
    nodes = block_count * size
    frames = readings_ref.shape[0]
    own = smooth_ref.shape[0]
    width = smooth_ref.shape[1]
    segments = frames // own

    hit_t = (
        lax.broadcasted_iota(jnp.int32, (nodes, index_ref.shape[1]), 0) == index_ref[...]
    ).astype(F32)
    gained = hit_t * gain_ref[...]
    damp_col = 1.0 - jnp.sum(gained, axis=1, keepdims=True)
    damp_row = 1.0 - jnp.sum(jnp.transpose(gained), axis=0, keepdims=True)
    inverse_damp = 1.0 / damp_row
    inject_ref[...] = lax.dot_general(
        readings_ref[...] * gain_ref[...], hit_t, NT,
        precision=lax.Precision.HIGHEST, preferred_element_type=F32,
    )

    keep_col = column(retention_ref[...])
    for row in range(block_count):
        rows = slice(row * size, (row + 1) * size)
        parts = [blocks_ref[row, band] for band in range(bands)]
        total = jnp.sum(functools.reduce(jnp.add, parts), axis=1, keepdims=True)
        factor = damp_col[rows] * (1.0 - keep_col[rows, :1]) / total
        parts = [part * factor for part in parts]
        for col in range(block_count):
            placed = jnp.zeros((size, size), F32)
            for band in range(bands):
                placed += jnp.where(offsets_ref[row, band] == col, parts[band], 0.0)
            spread_ref[rows, col * size : (col + 1) * size] = placed
    left_ref[...] = spread_ref[...].astype(BF16)
    right_ref[...] = jnp.transpose(spread_ref[...]).astype(BF16)
    diag_row = damp_row * retention_ref[...]
    diag_col = column(diag_row)[:, :1]

    extra = cov_half.shape[0] - nodes
    extra_row = lax.broadcasted_iota(jnp.int32, (extra, nodes), 0)

    def mean_rows(mean):
        low = mean - mean.astype(BF16).astype(F32)
        return jnp.where(extra_row == 0, mean, jnp.where(extra_row == 1, low, 0.0)).astype(BF16)

    def mean_step(frame, mean, spread_mean):
        scale_row = scale_rows_ref[pl.ds(frame, 1), :]
        moved = scale_row * (diag_row * mean + spread_mean)
        pred = moved * inverse_damp
        mean = moved + inject_ref[pl.ds(frame, 1), :]
        pred_ref[pl.ds(frame, 1), :] = pred
        innov_ref[pl.ds(frame, 1), :] = mean - pred
        return mean

    cov_now[...] = jnp.zeros_like(cov_now)
    cov_half[...] = jnp.zeros_like(cov_half)
    chunk = 256
    chunks = [slice(at, at + chunk) for at in range(0, nodes, chunk)]

    def full_frame(frame, mean):
        cov_half[nodes:, :] = mean_rows(mean)
        half = cov_half[...]
        firsts = []
        spread_mean = []
        for cols in chunks:
            product = dot(half, right_ref[:, cols])
            firsts.append(product[:nodes] + cov_now[:, cols] * diag_row[:, cols])
            spread_mean.append(product[nodes : nodes + 1] + product[nodes + 1 : nodes + 2])
        for cols, first in zip(chunks, firsts):
            second = dot(left_ref[...], first.astype(BF16)) + diag_col * first
            scale_row = scale_rows_ref[pl.ds(frame, 1), cols]
            for row in range(block_count):
                rows = slice(row * size, (row + 1) * size)
                both = scale_row * scale_ref[frame, row]
                value = second[rows] * both + noise_ref[rows, cols]
                cov_now[rows, cols] = value
                cov_half[rows, cols] = value.astype(BF16)
        return mean_step(frame, mean, jnp.concatenate(spread_mean, axis=1))

    def mean_frame(frame, mean):
        product = dot(mean_rows(mean), right_ref[...])
        return mean_step(frame, mean, product[0:1] + product[1:2])

    def segment_of(step):
        def body(index, mean):
            for offset in range(own):
                mean = step(index * own + offset, mean)
            return mean

        return body

    mean = lax.fori_loop(0, segment + 1, segment_of(full_frame), start_ref[...])
    cov_ref[0] = cov_now[:, pl.ds(pl.multiple_of(panel * width, width), width)]
    lax.fori_loop(segment + 1, segments, segment_of(mean_frame), mean)

    innov_ref[frames:, :] = jnp.zeros((frames, nodes), F32)
    power_ref[...] = smoother_ref[...]
    step = 1
    while step < frames:
        high, low = split(power_ref[...])
        later_high, later_low = split(innov_ref[pl.ds(step, frames), :])
        moved = dot_nt(later_high, high) + (dot_nt(later_high, low) + dot_nt(later_low, high))
        innov_ref[:frames, :] = innov_ref[:frames, :] + moved
        step *= 2
        if step < frames:
            power_ref[...] = dot(high, high) + (dot(high, low) + dot(low, high))
    lanes = pl.ds(pl.multiple_of(panel * width, width), width)
    for offset in range(own):
        at = pl.ds(segment * own + offset, 1)
        smooth_ref[offset : offset + 1, :] = pred_ref[at, lanes] + innov_ref[at, lanes]


def local(
    band_blocks,
    band_offsets,
    retention,
    frame_scale,
    sensor_index,
    sensor_gain,
    readings,
    noise_cov,
    initial_mean,
    smoother_gain,
):
    nodes = retention.shape[0]
    size = band_blocks.shape[2]
    own = readings.shape[0]
    width = noise_cov.shape[1]
    scales = lax.all_gather(frame_scale, "tm", axis=0, tiled=True)
    all_readings = lax.all_gather(readings, "tm", axis=0, tiled=True)
    noise = lax.all_gather(noise_cov, "rows", axis=1, tiled=True)
    frames = scales.shape[0]
    where = jnp.stack([lax.axis_index("tm"), lax.axis_index("rows")]).astype(jnp.int32)
    smem = pl.BlockSpec(memory_space=pltpu.SMEM)
    vmem = pl.BlockSpec(memory_space=pltpu.VMEM)
    return pl.pallas_call(
        kernel,
        out_shape=(
            jax.ShapeDtypeStruct((1, nodes, width), F32),
            jax.ShapeDtypeStruct((own, width), F32),
        ),
        in_specs=[smem] * 3 + [vmem] * 9,
        out_specs=(vmem, vmem),
        scratch_shapes=[
            pltpu.VMEM((nodes, nodes), F32),
            pltpu.VMEM((nodes, nodes), BF16),
            pltpu.VMEM((nodes, nodes), BF16),
            pltpu.VMEM((nodes, nodes), F32),
            pltpu.VMEM((nodes + 16, nodes), BF16),
            pltpu.VMEM((frames, nodes), F32),
            pltpu.VMEM((frames, nodes), F32),
            pltpu.VMEM((2 * frames, nodes), F32),
            pltpu.VMEM((nodes, nodes), F32),
        ],
        compiler_params=pltpu.CompilerParams(vmem_limit_bytes=48 * 1024 * 1024),
    )(
        where, band_offsets, scales, band_blocks, retention[None], sensor_index[None],
        sensor_gain[None], jnp.repeat(scales, size, axis=1), all_readings, noise,
        initial_mean[None], smoother_gain,
    )


def solution(mesh):
    return jax.shard_map(
        local,
        mesh=mesh,
        in_specs=(P(), P(), P(), P("tm", None), P(), P(), P("tm", None), P(None, "rows"), P(), P()),
        out_specs=(P("tm", None, "rows"), P("tm", "rows")),
        check_vma=False,
    )
```

```python
import functools

import jax
import jax.numpy as jnp
from jax import lax
from jax.experimental import pallas as pl
from jax.experimental.pallas import tpu as pltpu
from jax.sharding import PartitionSpec as P

F32 = jnp.float32
BF16 = jnp.bfloat16
NT = (((1,), (1,)), ((), ()))


def dot(left, right):
    return jnp.dot(left, right, preferred_element_type=F32)


def dot_nt(left, right):
    return lax.dot_general(left, right, NT, preferred_element_type=F32)


def split(value):
    high = value.astype(BF16)
    return high, (value - high.astype(F32)).astype(BF16)


def column(row, width=128):
    return jnp.transpose(jnp.broadcast_to(row, (width, row.shape[1])))


def gather_kernel(
    scale_ref, readings_ref, noise_ref,
    scales_ref, scale_rows_ref, all_readings_ref, whole_noise_ref,
    packed, landed, panels, send_sems, recv_sems, panel_sems,
):
    segment, panel = lax.axis_index("tm"), lax.axis_index("rows")
    segments = landed.shape[0]
    own, sensors = readings_ref.shape
    count = scale_ref.shape[1]
    width = noise_ref.shape[1]
    mesh_id = pl.DeviceIdType.MESH

    barrier = pltpu.get_barrier_semaphore()
    pl.semaphore_signal(barrier, inc=1, device_id=(segment, 1 - panel), device_id_type=mesh_id)

    def greet(step, carry):
        peer = lax.rem(segment + step, segments)
        pl.semaphore_signal(barrier, inc=1, device_id=(peer, panel), device_id_type=mesh_id)
        return carry

    lax.fori_loop(1, segments, greet, 0)
    packed[...] = jnp.zeros_like(packed)
    packed[:, :sensors] = readings_ref[...]
    packed[:, sensors : sensors + count] = scale_ref[...]
    pl.semaphore_wait(barrier, segments)

    def panel_copy():
        return pltpu.make_async_remote_copy(
            src_ref=noise_ref, dst_ref=panels, send_sem=panel_sems.at[0],
            recv_sem=panel_sems.at[1], device_id=(segment, 1 - panel), device_id_type=mesh_id,
        )

    def segment_copy(peer, slot, sem):
        return pltpu.make_async_remote_copy(
            src_ref=packed, dst_ref=landed.at[slot], send_sem=send_sems.at[sem],
            recv_sem=recv_sems.at[slot], device_id=(peer, panel), device_id_type=mesh_id,
        )

    def send(step, carry):
        segment_copy(lax.rem(segment + step, segments), segment, step).start()
        return carry

    lax.fori_loop(1, segments, send, 0)
    panel_copy().start()
    landed[segment] = packed[...]
    whole_noise_ref[:, pl.ds(pl.multiple_of(panel * width, width), width)] = noise_ref[...]

    def arrive(step, carry):
        source = lax.rem(segment + step, segments)
        copy = segment_copy(source, source, step)
        copy.wait_recv()
        copy.wait_send()
        return carry

    lax.fori_loop(1, segments, arrive, 0)
    for index in range(segments):
        rows = slice(index * own, (index + 1) * own)
        got = landed[index]
        all_readings_ref[rows, :] = got[:, :sensors]
        scales = got[:, sensors : sensors + count]
        scales_ref[rows, :] = scales
        nodes = scale_rows_ref.shape[1]
        block = lax.broadcasted_iota(jnp.int32, (own, nodes), 1) // (nodes // count)
        spread = jnp.zeros((own, nodes), F32)
        for col in range(count):
            spread = jnp.where(block == col, scales[:, col : col + 1], spread)
        scale_rows_ref[rows, :] = spread
    copy = panel_copy()
    copy.wait_recv()
    copy.wait_send()
    whole_noise_ref[:, pl.ds(pl.multiple_of((1 - panel) * width, width), width)] = panels[...]


def kernel(
    where_ref, offsets_ref, scale_ref, blocks_ref, retention_ref, index_ref, gain_ref,
    scale_rows_ref, readings_ref, noise_ref, start_ref, smoother_ref,
    cov_ref, smooth_ref,
    spread_ref, left_ref, right_ref, cov_now, cov_half, inject_ref, pred_ref, innov_ref,
    power_ref,
):
    segment, panel = where_ref[0], where_ref[1]
    block_count, bands, size, _ = blocks_ref.shape
    nodes = block_count * size
    frames = readings_ref.shape[0]
    own = smooth_ref.shape[0]
    width = smooth_ref.shape[1]
    segments = frames // own

    hit_t = (
        lax.broadcasted_iota(jnp.int32, (nodes, index_ref.shape[1]), 0) == index_ref[...]
    ).astype(F32)
    gained = hit_t * gain_ref[...]
    damp_col = 1.0 - jnp.sum(gained, axis=1, keepdims=True)
    damp_row = 1.0 - jnp.sum(jnp.transpose(gained), axis=0, keepdims=True)
    inverse_damp = 1.0 / damp_row
    inject_ref[...] = lax.dot_general(
        readings_ref[...] * gain_ref[...], hit_t, NT,
        precision=lax.Precision.HIGHEST, preferred_element_type=F32,
    )

    keep_col = column(retention_ref[...])
    for row in range(block_count):
        rows = slice(row * size, (row + 1) * size)
        parts = [blocks_ref[row, band] for band in range(bands)]
        total = jnp.sum(functools.reduce(jnp.add, parts), axis=1, keepdims=True)
        factor = damp_col[rows] * (1.0 - keep_col[rows, :1]) / total
        parts = [part * factor for part in parts]
        for col in range(block_count):
            placed = jnp.zeros((size, size), F32)
            for band in range(bands):
                placed += jnp.where(offsets_ref[row, band] == col, parts[band], 0.0)
            spread_ref[rows, col * size : (col + 1) * size] = placed
    left_ref[...] = spread_ref[...].astype(BF16)
    right_ref[...] = jnp.transpose(spread_ref[...]).astype(BF16)
    diag_row = damp_row * retention_ref[...]
    diag_col = column(diag_row)
    diag_col = jnp.concatenate([diag_col, diag_col], axis=1)

    extra = cov_half.shape[0] - nodes
    extra_row = lax.broadcasted_iota(jnp.int32, (extra, nodes), 0)

    def mean_rows(mean):
        low = mean - mean.astype(BF16).astype(F32)
        return jnp.where(extra_row == 0, mean, jnp.where(extra_row == 1, low, 0.0)).astype(BF16)

    def mean_step(frame, mean, spread_mean):
        scale_row = scale_rows_ref[pl.ds(frame, 1), :]
        moved = scale_row * (diag_row * mean + spread_mean)
        pred = moved * inverse_damp
        mean = moved + inject_ref[pl.ds(frame, 1), :]
        pred_ref[pl.ds(frame, 1), :] = pred
        innov_ref[pl.ds(frame, 1), :] = mean - pred
        return mean

    chunk = 256
    chunks = [slice(at, at + chunk) for at in range(0, nodes, chunk)]

    def full_frame(frame, mean):
        cov_half[nodes:, :] = mean_rows(mean)
        half = cov_half[...]
        firsts = []
        spread_mean = []
        for cols in chunks:
            product = dot(half, right_ref[:, cols])
            firsts.append(product[:nodes] + cov_now[:, cols] * diag_row[:, cols])
            spread_mean.append(product[nodes : nodes + 1] + product[nodes + 1 : nodes + 2])
        for cols, first in zip(chunks, firsts):
            second = dot(left_ref[...], first.astype(BF16)) + diag_col * first
            scale_row = scale_rows_ref[pl.ds(frame, 1), cols]
            for row in range(block_count):
                rows = slice(row * size, (row + 1) * size)
                both = scale_row * scale_ref[frame, row]
                value = second[rows] * both + noise_ref[rows, cols]
                cov_now[rows, cols] = value
                cov_half[rows, cols] = value.astype(BF16)
        return mean_step(frame, mean, jnp.concatenate(spread_mean, axis=1))

    def mean_frame(frame, mean):
        product = dot(mean_rows(mean), right_ref[...])
        return mean_step(frame, mean, product[0:1] + product[1:2])

    def segment_of(step):
        def body(index, mean):
            for offset in range(own):
                mean = step(index * own + offset, mean)
            return mean

        return body

    mean = mean_frame(0, start_ref[...])
    cov_now[...] = noise_ref[...]
    cov_half[:nodes, :] = noise_ref[...].astype(BF16)
    mean = lax.fori_loop(1, own, full_frame, mean)
    mean = lax.fori_loop(1, segment + 1, segment_of(full_frame), mean)
    cov_ref[0] = cov_now[:, pl.ds(pl.multiple_of(panel * width, width), width)]
    lax.fori_loop(segment + 1, segments, segment_of(mean_frame), mean)

    innov_ref[frames:, :] = jnp.zeros((frames, nodes), F32)
    power_ref[...] = smoother_ref[...]
    left = frames - segment * own

    def double(step):
        later_high, later_low = split(innov_ref[pl.ds(step, frames), :])
        if step > 1:
            before_high, before_low = split(power_ref[...])
            power_ref[...] = dot(before_high, before_high) + (
                dot(before_high, before_low) + dot(before_low, before_high)
            )
        high, low = split(power_ref[...])
        moved = dot_nt(later_high, high) + (dot_nt(later_high, low) + dot_nt(later_low, high))
        innov_ref[:frames, :] = innov_ref[:frames, :] + moved

    step = 1
    while step < frames:
        pl.when(step < left)(functools.partial(double, step))
        step *= 2
    lanes = pl.ds(pl.multiple_of(panel * width, width), width)
    for offset in range(own):
        at = pl.ds(segment * own + offset, 1)
        smooth_ref[offset : offset + 1, :] = pred_ref[at, lanes] + innov_ref[at, lanes]


def local(
    band_blocks,
    band_offsets,
    retention,
    frame_scale,
    sensor_index,
    sensor_gain,
    readings,
    noise_cov,
    initial_mean,
    smoother_gain,
):
    nodes = retention.shape[0]
    own = readings.shape[0]
    width = noise_cov.shape[1]
    segments = lax.axis_size("tm")
    vmem = pl.BlockSpec(memory_space=pltpu.VMEM)
    total = segments * own
    sensors = readings.shape[1]
    packed_width = sensors + 128
    scales, scale_rows, all_readings, noise = pl.pallas_call(
        gather_kernel,
        out_shape=(
            jax.ShapeDtypeStruct((total, frame_scale.shape[1]), F32),
            jax.ShapeDtypeStruct((total, nodes), F32),
            jax.ShapeDtypeStruct((total, sensors), F32),
            jax.ShapeDtypeStruct((nodes, nodes), F32),
        ),
        in_specs=[vmem] * 3,
        out_specs=(vmem,) * 4,
        scratch_shapes=[
            pltpu.VMEM((own, packed_width), F32),
            pltpu.VMEM((segments, own, packed_width), F32),
            pltpu.VMEM((nodes, width), F32),
            pltpu.SemaphoreType.DMA((segments,)),
            pltpu.SemaphoreType.DMA((segments,)),
            pltpu.SemaphoreType.DMA((2,)),
        ],
        compiler_params=pltpu.CompilerParams(
            collective_id=0, has_side_effects=True, vmem_limit_bytes=16 * 1024 * 1024
        ),
    )(frame_scale, readings, noise_cov)
    frames = scales.shape[0]
    where = jnp.stack([lax.axis_index("tm"), lax.axis_index("rows")]).astype(jnp.int32)
    smem = pl.BlockSpec(memory_space=pltpu.SMEM)
    return pl.pallas_call(
        kernel,
        out_shape=(
            jax.ShapeDtypeStruct((1, nodes, width), F32),
            jax.ShapeDtypeStruct((own, width), F32),
        ),
        in_specs=[smem] * 3 + [vmem] * 9,
        out_specs=(vmem, vmem),
        scratch_shapes=[
            pltpu.VMEM((nodes, nodes), F32),
            pltpu.VMEM((nodes, nodes), BF16),
            pltpu.VMEM((nodes, nodes), BF16),
            pltpu.VMEM((nodes, nodes), F32),
            pltpu.VMEM((nodes + 16, nodes), BF16),
            pltpu.VMEM((frames, nodes), F32),
            pltpu.VMEM((frames, nodes), F32),
            pltpu.VMEM((2 * frames, nodes), F32),
            pltpu.VMEM((nodes, nodes), F32),
        ],
        compiler_params=pltpu.CompilerParams(vmem_limit_bytes=48 * 1024 * 1024),
    )(
        where, band_offsets, scales, band_blocks, retention[None], sensor_index[None],
        sensor_gain[None], scale_rows, all_readings, noise,
        initial_mean[None], smoother_gain,
    )


def solution(mesh):
    return jax.shard_map(
        local,
        mesh=mesh,
        in_specs=(P(), P(), P(), P("tm", None), P(), P(), P("tm", None), P(None, "rows"), P(), P()),
        out_specs=(P("tm", None, "rows"), P("tm", "rows")),
        check_vma=False,
    )
```

```python
import functools

import jax
import jax.numpy as jnp
from jax import lax
from jax.experimental import pallas as pl
from jax.experimental.pallas import tpu as pltpu
from jax.sharding import PartitionSpec as P

F32 = jnp.float32
BF16 = jnp.bfloat16
NT = (((1,), (1,)), ((), ()))


def dot(left, right):
    return jnp.dot(left, right, preferred_element_type=F32)


def dot_nt(left, right):
    return lax.dot_general(left, right, NT, preferred_element_type=F32)


def split(value):
    high = value.astype(BF16)
    return high, (value - high.astype(F32)).astype(BF16)


def column(row, width=128):
    return jnp.transpose(jnp.broadcast_to(row, (width, row.shape[1])))


def gather_kernel(
    scale_ref, readings_ref, noise_ref,
    scales_ref, scale_rows_ref, all_readings_ref, whole_noise_ref,
    packed, landed, panels, send_sems, recv_sems, panel_sems,
):
    segment, panel = lax.axis_index("tm"), lax.axis_index("rows")
    segments = landed.shape[0]
    own, sensors = readings_ref.shape
    count = scale_ref.shape[1]
    width = noise_ref.shape[1]
    mesh_id = pl.DeviceIdType.MESH

    barrier = pltpu.get_barrier_semaphore()
    pl.semaphore_signal(barrier, inc=1, device_id=(segment, 1 - panel), device_id_type=mesh_id)

    def greet(step, carry):
        peer = lax.rem(segment + step, segments)
        pl.semaphore_signal(barrier, inc=1, device_id=(peer, panel), device_id_type=mesh_id)
        return carry

    lax.fori_loop(1, segments, greet, 0)
    packed[...] = jnp.zeros_like(packed)
    packed[:, :sensors] = readings_ref[...]
    packed[:, sensors : sensors + count] = scale_ref[...]
    pl.semaphore_wait(barrier, segments)

    def panel_copy():
        return pltpu.make_async_remote_copy(
            src_ref=noise_ref, dst_ref=panels, send_sem=panel_sems.at[0],
            recv_sem=panel_sems.at[1], device_id=(segment, 1 - panel), device_id_type=mesh_id,
        )

    def segment_copy(peer, slot, sem):
        return pltpu.make_async_remote_copy(
            src_ref=packed, dst_ref=landed.at[slot], send_sem=send_sems.at[sem],
            recv_sem=recv_sems.at[slot], device_id=(peer, panel), device_id_type=mesh_id,
        )

    def send(step, carry):
        segment_copy(lax.rem(segment + step, segments), segment, step).start()
        return carry

    lax.fori_loop(1, segments, send, 0)
    panel_copy().start()
    landed[segment] = packed[...]
    whole_noise_ref[:, pl.ds(pl.multiple_of(panel * width, width), width)] = noise_ref[...]

    def arrive(step, carry):
        source = lax.rem(segment + step, segments)
        copy = segment_copy(source, source, step)
        copy.wait_recv()
        copy.wait_send()
        return carry

    lax.fori_loop(1, segments, arrive, 0)
    for index in range(segments):
        rows = slice(index * own, (index + 1) * own)
        got = landed[index]
        all_readings_ref[rows, :] = got[:, :sensors]
        scales = got[:, sensors : sensors + count]
        scales_ref[rows, :] = scales
        nodes = scale_rows_ref.shape[1]
        block = lax.broadcasted_iota(jnp.int32, (own, nodes), 1) // (nodes // count)
        spread = jnp.zeros((own, nodes), F32)
        for col in range(count):
            spread = jnp.where(block == col, scales[:, col : col + 1], spread)
        scale_rows_ref[rows, :] = spread
    copy = panel_copy()
    copy.wait_recv()
    copy.wait_send()
    whole_noise_ref[:, pl.ds(pl.multiple_of((1 - panel) * width, width), width)] = panels[...]


def kernel(
    where_ref, offsets_ref, scale_ref, blocks_ref, retention_ref, index_ref, gain_ref,
    scale_rows_ref, readings_ref, noise_ref, start_ref, smoother_ref,
    cov_ref, smooth_ref,
    spread_ref, left_ref, right_ref, cov_now, cov_half, inject_ref, pred_ref, innov_ref,
    power_ref, smoother_sem,
):
    segment, panel = where_ref[0], where_ref[1]
    block_count, bands, size, _ = blocks_ref.shape
    nodes = block_count * size
    frames = readings_ref.shape[0]
    own = smooth_ref.shape[0]
    width = smooth_ref.shape[1]
    segments = frames // own

    smoother_copy = pltpu.make_async_copy(smoother_ref, power_ref, smoother_sem)
    smoother_copy.start()

    hit_t = (
        lax.broadcasted_iota(jnp.int32, (nodes, index_ref.shape[1]), 0) == index_ref[...]
    ).astype(F32)
    gained = hit_t * gain_ref[...]
    damp_col = 1.0 - jnp.sum(gained, axis=1, keepdims=True)
    damp_row = 1.0 - jnp.sum(jnp.transpose(gained), axis=0, keepdims=True)
    inverse_damp = 1.0 / damp_row
    inject_ref[...] = lax.dot_general(
        readings_ref[...] * gain_ref[...], hit_t, NT,
        precision=lax.Precision.HIGHEST, preferred_element_type=F32,
    )

    keep_col = column(retention_ref[...])
    for row in range(block_count):
        rows = slice(row * size, (row + 1) * size)
        parts = [blocks_ref[row, band] for band in range(bands)]
        total = jnp.sum(functools.reduce(jnp.add, parts), axis=1, keepdims=True)
        factor = damp_col[rows] * (1.0 - keep_col[rows, :1]) / total
        parts = [part * factor for part in parts]
        for col in range(block_count):
            placed = jnp.zeros((size, size), F32)
            for band in range(bands):
                placed += jnp.where(offsets_ref[row, band] == col, parts[band], 0.0)
            spread_ref[rows, col * size : (col + 1) * size] = placed
    left_ref[...] = spread_ref[...].astype(BF16)
    right_ref[...] = jnp.transpose(spread_ref[...]).astype(BF16)
    diag_row = damp_row * retention_ref[...]
    diag_col = column(diag_row)
    diag_col = jnp.concatenate([diag_col, diag_col], axis=1)

    extra = cov_half.shape[0] - nodes
    extra_row = lax.broadcasted_iota(jnp.int32, (extra, nodes), 0)

    def mean_rows(mean):
        low = mean - mean.astype(BF16).astype(F32)
        return jnp.where(extra_row == 0, mean, jnp.where(extra_row == 1, low, 0.0)).astype(BF16)

    def mean_step(frame, mean, spread_mean):
        scale_row = scale_rows_ref[pl.ds(frame, 1), :]
        moved = scale_row * (diag_row * mean + spread_mean)
        pred = moved * inverse_damp
        mean = moved + inject_ref[pl.ds(frame, 1), :]
        pred_ref[pl.ds(frame, 1), :] = pred
        innov_ref[pl.ds(frame, 1), :] = mean - pred
        return mean

    chunk = 256
    chunks = [slice(at, at + chunk) for at in range(0, nodes, chunk)]

    def full_frame(frame, mean):
        cov_half[nodes:, :] = mean_rows(mean)
        half = cov_half[...]
        firsts = []
        spread_mean = []
        for cols in chunks:
            product = dot(half, right_ref[:, cols])
            firsts.append(product[:nodes] + cov_now[:, cols] * diag_row[:, cols])
            spread_mean.append(product[nodes : nodes + 1] + product[nodes + 1 : nodes + 2])
        for cols, first in zip(chunks, firsts):
            second = dot(left_ref[...], first.astype(BF16)) + diag_col * first
            scale_row = scale_rows_ref[pl.ds(frame, 1), cols]
            for row in range(block_count):
                rows = slice(row * size, (row + 1) * size)
                both = scale_row * scale_ref[frame, row]
                value = second[rows] * both + noise_ref[rows, cols]
                cov_now[rows, cols] = value
                cov_half[rows, cols] = value.astype(BF16)
        return mean_step(frame, mean, jnp.concatenate(spread_mean, axis=1))

    def mean_frame(frame, mean):
        product = dot(mean_rows(mean), right_ref[...])
        return mean_step(frame, mean, product[0:1] + product[1:2])

    def segment_of(step):
        def body(index, mean):
            for offset in range(own):
                mean = step(index * own + offset, mean)
            return mean

        return body

    mean = mean_frame(0, start_ref[...])
    cov_now[...] = noise_ref[...]
    cov_half[:nodes, :] = noise_ref[...].astype(BF16)
    mean = lax.fori_loop(1, own, full_frame, mean)
    mean = lax.fori_loop(1, segment + 1, segment_of(full_frame), mean)
    cov_ref[0] = cov_now[:, pl.ds(pl.multiple_of(panel * width, width), width)]
    lax.fori_loop(segment + 1, segments, segment_of(mean_frame), mean)

    innov_ref[frames:, :] = jnp.zeros((frames, nodes), F32)
    smoother_copy.wait()
    left = frames - segment * own

    def double(step):
        later_high, later_low = split(innov_ref[pl.ds(step, frames), :])
        if step > 1:
            before_high, before_low = split(power_ref[...])
            power_ref[...] = dot(before_high, before_high) + (
                dot(before_high, before_low) + dot(before_low, before_high)
            )
        high, low = split(power_ref[...])
        moved = dot_nt(later_high, high) + (dot_nt(later_high, low) + dot_nt(later_low, high))
        innov_ref[:frames, :] = innov_ref[:frames, :] + moved

    step = 1
    while step < frames:
        pl.when(step < left)(functools.partial(double, step))
        step *= 2
    lanes = pl.ds(pl.multiple_of(panel * width, width), width)
    for offset in range(own):
        at = pl.ds(segment * own + offset, 1)
        smooth_ref[offset : offset + 1, :] = pred_ref[at, lanes] + innov_ref[at, lanes]


def local(
    band_blocks,
    band_offsets,
    retention,
    frame_scale,
    sensor_index,
    sensor_gain,
    readings,
    noise_cov,
    initial_mean,
    smoother_gain,
):
    nodes = retention.shape[0]
    own = readings.shape[0]
    width = noise_cov.shape[1]
    segments = lax.axis_size("tm")
    vmem = pl.BlockSpec(memory_space=pltpu.VMEM)
    total = segments * own
    sensors = readings.shape[1]
    packed_width = sensors + 128
    scales, scale_rows, all_readings, noise = pl.pallas_call(
        gather_kernel,
        out_shape=(
            jax.ShapeDtypeStruct((total, frame_scale.shape[1]), F32),
            jax.ShapeDtypeStruct((total, nodes), F32),
            jax.ShapeDtypeStruct((total, sensors), F32),
            jax.ShapeDtypeStruct((nodes, nodes), F32),
        ),
        in_specs=[vmem] * 3,
        out_specs=(vmem,) * 4,
        scratch_shapes=[
            pltpu.VMEM((own, packed_width), F32),
            pltpu.VMEM((segments, own, packed_width), F32),
            pltpu.VMEM((nodes, width), F32),
            pltpu.SemaphoreType.DMA((segments,)),
            pltpu.SemaphoreType.DMA((segments,)),
            pltpu.SemaphoreType.DMA((2,)),
        ],
        compiler_params=pltpu.CompilerParams(
            collective_id=0, has_side_effects=True, vmem_limit_bytes=16 * 1024 * 1024
        ),
    )(frame_scale, readings, noise_cov)
    frames = scales.shape[0]
    where = jnp.stack([lax.axis_index("tm"), lax.axis_index("rows")]).astype(jnp.int32)
    smem = pl.BlockSpec(memory_space=pltpu.SMEM)
    return pl.pallas_call(
        kernel,
        out_shape=(
            jax.ShapeDtypeStruct((1, nodes, width), F32),
            jax.ShapeDtypeStruct((own, width), F32),
        ),
        in_specs=[smem] * 3 + [vmem] * 8 + [pl.BlockSpec(memory_space=pl.ANY)],
        out_specs=(vmem, vmem),
        scratch_shapes=[
            pltpu.VMEM((nodes, nodes), F32),
            pltpu.VMEM((nodes, nodes), BF16),
            pltpu.VMEM((nodes, nodes), BF16),
            pltpu.VMEM((nodes, nodes), F32),
            pltpu.VMEM((nodes + 16, nodes), BF16),
            pltpu.VMEM((frames, nodes), F32),
            pltpu.VMEM((frames, nodes), F32),
            pltpu.VMEM((2 * frames, nodes), F32),
            pltpu.VMEM((nodes, nodes), F32),
            pltpu.SemaphoreType.DMA,
        ],
        compiler_params=pltpu.CompilerParams(vmem_limit_bytes=48 * 1024 * 1024),
    )(
        where, band_offsets, scales, band_blocks, retention[None], sensor_index[None],
        sensor_gain[None], scale_rows, all_readings, noise,
        initial_mean[None], smoother_gain,
    )


def solution(mesh):
    return jax.shard_map(
        local,
        mesh=mesh,
        in_specs=(P(), P(), P(), P("tm", None), P(), P(), P("tm", None), P(None, "rows"), P(), P()),
        out_specs=(P("tm", None, "rows"), P("tm", "rows")),
        check_vma=False,
    )
```

```python
import functools

import jax
import jax.numpy as jnp
from jax import lax
from jax.experimental import pallas as pl
from jax.experimental.pallas import tpu as pltpu
from jax.sharding import PartitionSpec as P

F32 = jnp.float32
BF16 = jnp.bfloat16
NT = (((1,), (1,)), ((), ()))


def dot(left, right):
    return jnp.dot(left, right, preferred_element_type=F32)


def dot_nt(left, right):
    return lax.dot_general(left, right, NT, preferred_element_type=F32)


def split(value):
    high = value.astype(BF16)
    return high, (value - high.astype(F32)).astype(BF16)


def column(row, width=128):
    return jnp.transpose(jnp.broadcast_to(row, (width, row.shape[1])))


def gather_kernel(
    scale_ref, readings_ref, noise_ref,
    scales_ref, scale_rows_ref, all_readings_ref, whole_noise_ref,
    packed, landed, panels, send_sems, recv_sems, panel_sems,
):
    segment, panel = lax.axis_index("tm"), lax.axis_index("rows")
    segments = landed.shape[0]
    own, sensors = readings_ref.shape
    count = scale_ref.shape[1]
    width = noise_ref.shape[1]
    mesh_id = pl.DeviceIdType.MESH

    barrier = pltpu.get_barrier_semaphore()
    pl.semaphore_signal(barrier, inc=1, device_id=(segment, 1 - panel), device_id_type=mesh_id)

    def greet(step, carry):
        peer = lax.rem(segment + step, segments)
        pl.semaphore_signal(barrier, inc=1, device_id=(peer, panel), device_id_type=mesh_id)
        return carry

    lax.fori_loop(1, segments, greet, 0)
    packed[...] = jnp.zeros_like(packed)
    packed[:, :sensors] = readings_ref[...]
    packed[:, sensors : sensors + count] = scale_ref[...]
    pl.semaphore_wait(barrier, segments)

    def panel_copy():
        return pltpu.make_async_remote_copy(
            src_ref=noise_ref, dst_ref=panels, send_sem=panel_sems.at[0],
            recv_sem=panel_sems.at[1], device_id=(segment, 1 - panel), device_id_type=mesh_id,
        )

    def segment_copy(peer, slot, sem):
        return pltpu.make_async_remote_copy(
            src_ref=packed, dst_ref=landed.at[slot], send_sem=send_sems.at[sem],
            recv_sem=recv_sems.at[slot], device_id=(peer, panel), device_id_type=mesh_id,
        )

    def send(step, carry):
        segment_copy(lax.rem(segment + step, segments), segment, step).start()
        return carry

    lax.fori_loop(1, segments, send, 0)
    panel_copy().start()
    landed[segment] = packed[...]
    whole_noise_ref[:, pl.ds(pl.multiple_of(panel * width, width), width)] = noise_ref[...]

    def arrive(step, carry):
        source = lax.rem(segment + step, segments)
        copy = segment_copy(source, source, step)
        copy.wait_recv()
        copy.wait_send()
        return carry

    lax.fori_loop(1, segments, arrive, 0)
    for index in range(segments):
        rows = slice(index * own, (index + 1) * own)
        got = landed[index]
        all_readings_ref[rows, :] = got[:, :sensors]
        scales = got[:, sensors : sensors + count]
        scales_ref[rows, :] = scales
        nodes = scale_rows_ref.shape[1]
        block = lax.broadcasted_iota(jnp.int32, (own, nodes), 1) // (nodes // count)
        spread = jnp.zeros((own, nodes), F32)
        for col in range(count):
            spread = jnp.where(block == col, scales[:, col : col + 1], spread)
        scale_rows_ref[rows, :] = spread
    copy = panel_copy()
    copy.wait_recv()
    copy.wait_send()
    whole_noise_ref[:, pl.ds(pl.multiple_of((1 - panel) * width, width), width)] = panels[...]


def kernel(
    where_ref, offsets_ref, scale_ref, blocks_hbm, retention_ref, index_ref, gain_ref,
    scale_rows_ref, readings_ref, noise_ref, start_ref, smoother_ref,
    cov_ref, smooth_ref,
    spread_ref, left_ref, right_ref, cov_now, cov_half, inject_ref, pred_ref, innov_ref,
    power_ref, smoother_sem, blocks_ref, blocks_sem,
):
    segment, panel = where_ref[0], where_ref[1]
    block_count, bands, size, _ = blocks_ref.shape
    nodes = block_count * size
    frames = readings_ref.shape[0]
    own = smooth_ref.shape[0]
    width = smooth_ref.shape[1]
    segments = frames // own

    blocks_copy = pltpu.make_async_copy(blocks_hbm, blocks_ref, blocks_sem)
    blocks_copy.start()
    smoother_copy = pltpu.make_async_copy(smoother_ref, power_ref, smoother_sem)
    smoother_copy.start()

    hit_t = (
        lax.broadcasted_iota(jnp.int32, (nodes, index_ref.shape[1]), 0) == index_ref[...]
    ).astype(F32)
    gained = hit_t * gain_ref[...]
    damp_col = 1.0 - jnp.sum(gained, axis=1, keepdims=True)
    damp_row = 1.0 - jnp.sum(jnp.transpose(gained), axis=0, keepdims=True)
    inverse_damp = 1.0 / damp_row
    inject_ref[...] = lax.dot_general(
        readings_ref[...] * gain_ref[...], hit_t, NT,
        precision=lax.Precision.HIGHEST, preferred_element_type=F32,
    )

    blocks_copy.wait()
    keep_col = column(retention_ref[...])
    for row in range(block_count):
        rows = slice(row * size, (row + 1) * size)
        parts = [blocks_ref[row, band] for band in range(bands)]
        total = jnp.sum(functools.reduce(jnp.add, parts), axis=1, keepdims=True)
        factor = damp_col[rows] * (1.0 - keep_col[rows, :1]) / total
        parts = [part * factor for part in parts]
        for col in range(block_count):
            placed = jnp.zeros((size, size), F32)
            for band in range(bands):
                placed += jnp.where(offsets_ref[row, band] == col, parts[band], 0.0)
            spread_ref[rows, col * size : (col + 1) * size] = placed
    left_ref[...] = spread_ref[...].astype(BF16)
    right_ref[...] = jnp.transpose(spread_ref[...]).astype(BF16)
    diag_row = damp_row * retention_ref[...]
    diag_col = column(diag_row)
    diag_col = jnp.concatenate([diag_col, diag_col], axis=1)

    extra = cov_half.shape[0] - nodes
    extra_row = lax.broadcasted_iota(jnp.int32, (extra, nodes), 0)

    def mean_rows(mean):
        low = mean - mean.astype(BF16).astype(F32)
        return jnp.where(extra_row == 0, mean, jnp.where(extra_row == 1, low, 0.0)).astype(BF16)

    def mean_step(frame, mean, spread_mean):
        scale_row = scale_rows_ref[pl.ds(frame, 1), :]
        moved = scale_row * (diag_row * mean + spread_mean)
        pred = moved * inverse_damp
        mean = moved + inject_ref[pl.ds(frame, 1), :]
        pred_ref[pl.ds(frame, 1), :] = pred
        innov_ref[pl.ds(frame, 1), :] = mean - pred
        return mean

    chunk = 256
    chunks = [slice(at, at + chunk) for at in range(0, nodes, chunk)]

    def full_frame(frame, mean):
        cov_half[nodes:, :] = mean_rows(mean)
        half = cov_half[...]
        firsts = []
        spread_mean = []
        for cols in chunks:
            product = dot(half, right_ref[:, cols])
            firsts.append(product[:nodes] + cov_now[:, cols] * diag_row[:, cols])
            spread_mean.append(product[nodes : nodes + 1] + product[nodes + 1 : nodes + 2])
        for cols, first in zip(chunks, firsts):
            second = dot(left_ref[...], first.astype(BF16)) + diag_col * first
            scale_row = scale_rows_ref[pl.ds(frame, 1), cols]
            for row in range(block_count):
                rows = slice(row * size, (row + 1) * size)
                both = scale_row * scale_ref[frame, row]
                value = second[rows] * both + noise_ref[rows, cols]
                cov_now[rows, cols] = value
                cov_half[rows, cols] = value.astype(BF16)
        return mean_step(frame, mean, jnp.concatenate(spread_mean, axis=1))

    def mean_frame(frame, mean):
        product = dot(mean_rows(mean), right_ref[...])
        return mean_step(frame, mean, product[0:1] + product[1:2])

    def segment_of(step):
        def body(index, mean):
            for offset in range(own):
                mean = step(index * own + offset, mean)
            return mean

        return body

    mean = mean_frame(0, start_ref[...])
    cov_now[...] = noise_ref[...]
    cov_half[:nodes, :] = noise_ref[...].astype(BF16)
    mean = lax.fori_loop(1, own, full_frame, mean)
    mean = lax.fori_loop(1, segment + 1, segment_of(full_frame), mean)
    cov_ref[0] = cov_now[:, pl.ds(pl.multiple_of(panel * width, width), width)]
    lax.fori_loop(segment + 1, segments, segment_of(mean_frame), mean)

    innov_ref[frames:, :] = jnp.zeros((frames, nodes), F32)
    smoother_copy.wait()
    left = frames - segment * own

    def double(step):
        later_high, later_low = split(innov_ref[pl.ds(step, frames), :])
        if step > 1:
            before_high, before_low = split(power_ref[...])
            power_ref[...] = dot(before_high, before_high) + (
                dot(before_high, before_low) + dot(before_low, before_high)
            )
        high, low = split(power_ref[...])
        moved = dot_nt(later_high, high) + (dot_nt(later_high, low) + dot_nt(later_low, high))
        innov_ref[:frames, :] = innov_ref[:frames, :] + moved

    step = 1
    while step < frames:
        pl.when(step < left)(functools.partial(double, step))
        step *= 2
    lanes = pl.ds(pl.multiple_of(panel * width, width), width)
    for offset in range(own):
        at = pl.ds(segment * own + offset, 1)
        smooth_ref[offset : offset + 1, :] = pred_ref[at, lanes] + innov_ref[at, lanes]


def local(
    band_blocks,
    band_offsets,
    retention,
    frame_scale,
    sensor_index,
    sensor_gain,
    readings,
    noise_cov,
    initial_mean,
    smoother_gain,
):
    nodes = retention.shape[0]
    own = readings.shape[0]
    width = noise_cov.shape[1]
    segments = lax.axis_size("tm")
    vmem = pl.BlockSpec(memory_space=pltpu.VMEM)
    total = segments * own
    sensors = readings.shape[1]
    packed_width = sensors + 128
    scales, scale_rows, all_readings, noise = pl.pallas_call(
        gather_kernel,
        out_shape=(
            jax.ShapeDtypeStruct((total, frame_scale.shape[1]), F32),
            jax.ShapeDtypeStruct((total, nodes), F32),
            jax.ShapeDtypeStruct((total, sensors), F32),
            jax.ShapeDtypeStruct((nodes, nodes), F32),
        ),
        in_specs=[vmem] * 3,
        out_specs=(vmem,) * 4,
        scratch_shapes=[
            pltpu.VMEM((own, packed_width), F32),
            pltpu.VMEM((segments, own, packed_width), F32),
            pltpu.VMEM((nodes, width), F32),
            pltpu.SemaphoreType.DMA((segments,)),
            pltpu.SemaphoreType.DMA((segments,)),
            pltpu.SemaphoreType.DMA((2,)),
        ],
        compiler_params=pltpu.CompilerParams(
            collective_id=0, has_side_effects=True, vmem_limit_bytes=16 * 1024 * 1024
        ),
    )(frame_scale, readings, noise_cov)
    frames = scales.shape[0]
    where = jnp.stack([lax.axis_index("tm"), lax.axis_index("rows")]).astype(jnp.int32)
    smem = pl.BlockSpec(memory_space=pltpu.SMEM)
    return pl.pallas_call(
        kernel,
        out_shape=(
            jax.ShapeDtypeStruct((1, nodes, width), F32),
            jax.ShapeDtypeStruct((own, width), F32),
        ),
        in_specs=[smem] * 3 + [pl.BlockSpec(memory_space=pl.ANY)] + [vmem] * 7 + [pl.BlockSpec(memory_space=pl.ANY)],
        out_specs=(vmem, vmem),
        scratch_shapes=[
            pltpu.VMEM((nodes, nodes), F32),
            pltpu.VMEM((nodes, nodes), BF16),
            pltpu.VMEM((nodes, nodes), BF16),
            pltpu.VMEM((nodes, nodes), F32),
            pltpu.VMEM((nodes + 16, nodes), BF16),
            pltpu.VMEM((frames, nodes), F32),
            pltpu.VMEM((frames, nodes), F32),
            pltpu.VMEM((2 * frames, nodes), F32),
            pltpu.VMEM((nodes, nodes), F32),
            pltpu.SemaphoreType.DMA,
            pltpu.VMEM(band_blocks.shape, F32),
            pltpu.SemaphoreType.DMA,
        ],
        compiler_params=pltpu.CompilerParams(vmem_limit_bytes=48 * 1024 * 1024),
    )(
        where, band_offsets, scales, band_blocks, retention[None], sensor_index[None],
        sensor_gain[None], scale_rows, all_readings, noise,
        initial_mean[None], smoother_gain,
    )


def solution(mesh):
    return jax.shard_map(
        local,
        mesh=mesh,
        in_specs=(P(), P(), P(), P("tm", None), P(), P(), P("tm", None), P(None, "rows"), P(), P()),
        out_specs=(P("tm", None, "rows"), P("tm", "rows")),
        check_vma=False,
    )
```
